32 devices in a mesh: member: 8 (over y, x, core), tile: 4 (over z).
Axes of the slice: x: 2, y: 2, z: 4, core: 2. Of those that a mesh axis runs over, the one named last changes fastest.
Arguments:
- innovations: bfloat16 [8, 4, 256, 256], P('member', None, None, 'tile'), may hold values from -6 to 6
- obs_column: int32 [4, 256], P(None, 'tile'), may hold values from 0 to 511
- physics: float32 [4, 256, 256], replicated, as said below
- diffusion: float32 [256], replicated, may hold values from 0.05 to 0.24
- anomalies: bfloat16 [8, 256, 16, 128], P('member', None, 'tile'), may hold values from -6 to 6
- modes: float32 [256, 16], replicated, may hold values from -3 to 3
- bands: int32 [16], replicated, may hold values from 1 to 8
Outputs:
- gradient: float32 [8, 256, 16, 128], P('member', None, 'tile')
The draws below stay inside these ranges and needn't reach their ends.
Inputs may be any that keep to these rules, and one draw needn't show every extreme that they name: `obs_column`: index c = x * 128 + y of an observed column within its tile's 4 by 128 columns; indices may repeat. `physics`: each step's matrix has a dominant diagonal near 0.6.
All inputs are finite; a program needn't handle non-finite values.
Results may differ from the reference program's by a relative error of at most 0.0003.
Values sent between devices are 32-bit elements; how exact they have to be, the bound alone decides.
A program may use at most 64 MiB of HBM per device.

```python
import jax
import jax.numpy as jnp
from jax import lax

STATE = 256
MODES = 16
STEPS = 4
NY = 128
CX = 4
OBS = 64
MEMBERS = 8
NX = 16
N_TILE = 4


def draw_physics(key, part):
    inner = jax.random.fold_in(key, 17)
    noise = jax.random.normal(inner, (STEPS, STATE, STATE), jnp.float32)
    eye = jnp.eye(STATE, dtype=jnp.float32)[None]
    return 0.6 * eye + 0.4 * noise / jnp.sqrt(jnp.float32(STATE))


def set_ends(drawn, stream_key, least, top_value):
    longest = drawn.shape.index(max(drawn.shape))
    spots = []
    for shift in (0, 1):
        where = [jax.random.randint(jax.random.fold_in(stream_key, axis), (), 0, length) for axis, length in enumerate(drawn.shape)]
        where[longest] = (where[longest] + shift) % drawn.shape[longest]
        spots.append(tuple(where))
    return drawn.at[spots[0]].set(least).at[spots[1]].set(top_value)


def block_scale(rng, dims, cuts, low, top_value):
    factor_of = 1.0
    for position, blocks in cuts:
        heights = jax.random.uniform(jax.random.fold_in(jax.random.fold_in(rng, 6), position), (blocks,), jnp.float32, low / len(cuts), top_value / len(cuts))
        factor_of = factor_of * jnp.repeat(jnp.exp(heights), dims[position] // blocks).reshape((-1,) + (1,) * (len(dims) - 1 - position))
    return factor_of


def centred(key, extent, scale, bound, split=(), held_as=jnp.bfloat16):
    array = jax.random.normal(key, extent, jnp.float32) * scale
    if len(split) > 0:
        array = block_scale(key, extent, split, -0.22, 0.18) * array
    return jnp.clip(array, min=-bound, max=bound).astype(held_as)


def setup_inputs(seed: int = 0) -> dict:
    keys = jax.random.split(jax.random.key(seed), 8)
    return {
        "innovations": centred(keys[0], (MEMBERS, STEPS, STATE, N_TILE * OBS), 1.0, 6.0, ((0, 8), (3, 4))),
        "obs_column": set_ends(jax.random.randint(keys[1], (STEPS, N_TILE * OBS), 0, CX * NY), jax.random.fold_in(keys[1], 1), 0, (CX * NY) - 1).astype(jnp.int32),
        "physics": draw_physics(jax.random.fold_in(keys[7], 71), 0),
        "diffusion": jnp.clip(jax.random.uniform(keys[3], (STATE,), jnp.float32, 0.05, 0.24), 0.05, 0.24),
        "anomalies": centred(keys[4], (MEMBERS, STATE, NX, NY), 1.0, 6.0, ((0, 8), (2, 4))),
        "modes": centred(keys[5], (STATE, MODES), 0.5, 3.0, (), jnp.float32),
        "bands": set_ends(jax.random.randint(keys[6], (MODES,), 1, 9), jax.random.fold_in(keys[6], 1), 1, 8).astype(jnp.int32),
    }


def smooth_modes(coeffs, bands):
    length = coeffs.shape[-1]
    padded = jnp.pad(coeffs, ((0, 0), (0, 0), (8, 8)))
    total = jnp.zeros(coeffs.shape, jnp.float32)
    for offset in range(-8, 9):
        weight = (jnp.abs(jnp.int32(offset)) <= bands).astype(jnp.float32)
        total = total + weight[:, None, None] * padded[:, :, 8 + offset:8 + offset + length]
    return total / (2 * bands + 1).astype(jnp.float32)[:, None, None]


def reference(innovations, obs_column, physics, diffusion, anomalies, modes, bands):
    members = anomalies.shape[0]
    state = anomalies.shape[1]
    spread = anomalies.astype(jnp.float32)
    tiles = obs_column.shape[1] // OBS
    owner = (jnp.arange(tiles * OBS, dtype=jnp.int32) // OBS) * (CX * NY)
    lam = jnp.zeros(anomalies.shape, jnp.float32)
    nu = diffusion[None, :, None, None]
    for step in range(STEPS - 1, -1, -1):
        local = jnp.einsum("sk,msxy->mkxy", modes, spread * lam, precision=lax.Precision.HIGHEST)
        coeffs = jnp.sum(local, axis=0) / jnp.float32(members - 1)
        smooth = smooth_modes(coeffs, bands)
        lifted = jnp.einsum("sk,kxy->sxy", modes, smooth, precision=lax.Precision.HIGHEST)
        moved = jnp.einsum("rs,mrxy->msxy", physics[step], lam, precision=lax.Precision.HIGHEST)
        ypad = jnp.pad(moved, ((0, 0), (0, 0), (0, 0), (1, 1)))
        beside_all = jnp.roll(moved, 1, axis=2) + jnp.roll(moved, -1, axis=2) + ypad[..., 2:] + ypad[..., :-2]
        spread_out = moved + nu * (beside_all - 4.0 * moved)
        flat = owner + obs_column[step].astype(jnp.int32)
        forcing = jnp.zeros((members, state, NX * NY), jnp.float32)
        forcing = forcing.at[:, :, flat].add(innovations[:, step].astype(jnp.float32))
        forcing = forcing.reshape(members, state, NX, NY)
        lam = spread_out + spread * lifted[None] + forcing
    return lam
```

```python
import functools

import jax
import jax.numpy as jnp
from jax import lax
from jax.experimental import pallas as pl
from jax.experimental.pallas import tpu as pltpu
from jax.sharding import PartitionSpec as P

REACH = 8
MESH = pl.DeviceIdType.MESH
F32 = jnp.float32
BF16 = jnp.bfloat16


def split(x):
    hi = x.astype(BF16)
    return hi, (x - hi.astype(F32)).astype(BF16)


def dot(a, b):
    return jnp.dot(a, b, preferred_element_type=F32)


def stacked(x):
    hi, lo = split(x)
    return jnp.concatenate([hi, lo, hi], axis=0)


def spread_obs(profile, obs_row, first, count):
    shape = (count, obs_row.shape[-1])
    column = lax.broadcasted_iota(jnp.int32, shape, 0) + first
    onehot = jnp.where(column == obs_row, 1.0, 0.0).astype(BF16)
    return lax.dot_general(
        profile, onehot, (((0,), (1,)), ((), ())), preferred_element_type=F32
    )


def kernel(
    members, tiles, bands_ref, obs_ref, diff_ref, modes_ref, phys_ref, innov_ref, anom_ref,
    out_ref,
    phys, innov, anom, anom32, weight, field, nu_ref, lift_w, proj_w, smooth_w,
    edge, edge_obs, u_ref, q_ref, total,
    local_sem, edge_send, edge_recv, obs_send, obs_recv, u_send, u_recv, q_send, q_recv,
):
    steps, obs, state = innov.shape
    ny = anom.shape[1]
    nx = anom.shape[0] // state
    modes = modes_ref.shape[0]
    rounds = steps - 1
    me = lax.axis_index("member")
    tile = lax.axis_index("tile")
    after = lax.rem(tile + 1, tiles)
    before = lax.rem(tile + tiles - 1, tiles)

    get_innov = pltpu.make_async_copy(innov_ref.at[0], innov, local_sem.at[0])
    get_phys = pltpu.make_async_copy(phys_ref.at[pl.ds(0, rounds)], phys, local_sem.at[1])
    get_anom = pltpu.make_async_copy(anom_ref, anom, local_sem.at[2])
    get_innov.start()
    get_anom.start()
    get_phys.start()

    barrier = pltpu.get_barrier_semaphore()
    for near in (before, after):
        pl.semaphore_signal(barrier, inc=1, device_id={"tile": near}, device_id_type=MESH)
    for j in range(1, members):
        peer = lax.rem(me + j, members)
        pl.semaphore_signal(barrier, inc=1, device_id={"member": peer}, device_id_type=MESH)

    get_innov.wait()
    edge[0] = innov[rounds].astype(F32)
    pl.semaphore_wait(barrier, members + 1)

    edge_copies = []
    for side, near in ((0, after), (1, before)):
        edge_copies.append(pltpu.make_async_remote_copy(
            edge.at[0], edge.at[1 + side], edge_send.at[side], edge_recv.at[side],
            device_id={"tile": near}, device_id_type=MESH))
        edge_copies.append(pltpu.make_async_remote_copy(
            obs_ref, edge_obs.at[side], obs_send.at[side], obs_recv.at[side],
            device_id={"tile": near}, device_id_type=MESH))
    for copy in edge_copies:
        copy.start()

    obs_all = obs_ref[...]
    field[...] = spread_obs(innov[rounds], obs_all[rounds : rounds + 1], 0, nx * ny)

    hi, lo = split(modes_ref[...])
    proj_w[...] = jnp.concatenate([hi, lo], axis=0)
    parts = jnp.concatenate([hi, hi, lo], axis=0).astype(F32)
    pad = lift_w.shape[1] - 3 * modes
    lift_w[...] = jnp.concatenate([parts, jnp.zeros((pad, state), F32)], axis=0).T.astype(BF16)

    get_anom.wait()
    anom32[...] = anom[...].astype(F32)

    def project_and_send(r):
        hi_cols, lo_cols = [], []
        for x in range(nx):
            cols = slice(x * ny, (x + 1) * ny)
            a, b = split(anom32[pl.ds(x, state, stride=nx), :] * field[:, cols])
            hi_cols.append(a)
            lo_cols.append(b)
        both = dot(proj_w[...], jnp.concatenate(hi_cols, axis=1))
        low = dot(proj_w[0:modes], jnp.concatenate(lo_cols, axis=1))
        q_ref[r, 0] = both[0:modes] + both[modes:] + low
        copies = []
        for j in range(1, members):
            copies.append(pltpu.make_async_remote_copy(
                q_ref.at[r, 0], q_ref.at[r, j], q_send.at[r, j], q_recv.at[r, j],
                device_id={"member": lax.rem(me + j, members)}, device_id_type=MESH))
        for copy in copies:
            copy.start()
        return copies

    pending = project_and_send(0)

    row = lax.broadcasted_iota(jnp.int32, (modes, ny), 0)
    lane = lax.broadcasted_iota(jnp.int32, (modes, ny), 1)
    bands = jnp.zeros((modes, ny), jnp.int32)
    for k in range(modes):
        bands = jnp.where(row == k, bands_ref[k], bands)
    scale = 1.0 / ((2 * bands + 1).astype(F32) * F32(members - 1))
    for i, d in enumerate(range(-REACH, REACH + 1)):
        ok = (abs(d) <= bands) & (lane + d >= 0) & (lane + d < ny)
        smooth_w[i] = jnp.where(ok, scale, 0.0)

    nu_ref[...] = jnp.broadcast_to(diff_ref[...], (ny, state)).T

    get_phys.wait()

    def physics_weights(t):
        hi, lo = split(phys[t].T)
        weight[t] = jnp.concatenate([hi, hi, lo], axis=1)

    physics_weights(rounds - 1)

    def smoothed(r):
        rows = []
        for x in range(nx):
            cols = slice(x * ny, (x + 1) * ny)
            q = total[:, cols]
            acc = smooth_w[REACH] * q
            for i, d in enumerate(range(-REACH, REACH + 1)):
                if d != 0:
                    acc = acc + smooth_w[i] * pltpu.roll(q, (-d) % ny, 1)
            rows.append(acc)
        return jnp.concatenate(rows, axis=1)

    lane_y = lax.broadcasted_iota(jnp.int32, (state, ny), 1)

    for r in range(rounds):
        t = rounds - 1 - r
        halo = []
        if r > 0:
            outer = jnp.concatenate([field[:, 0:ny], field[:, (nx - 1) * ny :]], axis=1)
            u = dot(weight[t], stacked(outer))
            u_ref[r, 1] = u[:, 0:ny]
            u_ref[r, nx] = u[:, ny:]
            halo = [
                pltpu.make_async_remote_copy(
                    u_ref.at[r, 1], u_ref.at[r, nx + 1], u_send.at[r, 0], u_recv.at[r, 0],
                    device_id={"tile": before}, device_id_type=MESH),
                pltpu.make_async_remote_copy(
                    u_ref.at[r, nx], u_ref.at[r, 0], u_send.at[r, 1], u_recv.at[r, 1],
                    device_id={"tile": after}, device_id_type=MESH),
            ]
            for copy in halo:
                copy.start()
            pending = project_and_send(r)
            u = dot(weight[t], stacked(field[:, ny : (nx - 1) * ny]))
            for x in range(1, nx - 1):
                u_ref[r, 1 + x] = u[:, (x - 1) * ny : x * ny]
        else:
            u = dot(weight[t], stacked(field[...]))
            for x in range(nx):
                u_ref[r, 1 + x] = u[:, x * ny : (x + 1) * ny]
        if t > 0:
            physics_weights(t - 1)
        nu = nu_ref[...]
        field[...] = spread_obs(innov[t], obs_all[t : t + 1], 0, nx * ny)
        for x in range(nx):
            cols = slice(x * ny, (x + 1) * ny)
            mid = u_ref[r, 1 + x]
            beside = jnp.where(lane_y == 0, 0.0, pltpu.roll(mid, 1, 1))
            beside = beside + jnp.where(lane_y == ny - 1, 0.0, pltpu.roll(mid, ny - 1, 1))
            if x > 0:
                beside = beside + u_ref[r, x]
            if x < nx - 1:
                beside = beside + u_ref[r, x + 2]
            field[:, cols] += mid + nu * (beside - 4.0 * mid)
        if r == 0:
            for copy in edge_copies:
                copy.wait()
            last = (nx - 1) * ny
            low = spread_obs(edge[1].astype(BF16), edge_obs[0, rounds : rounds + 1], last, ny)
            high = spread_obs(edge[2].astype(BF16), edge_obs[1, rounds : rounds + 1], 0, ny)
            u = dot(weight[t], stacked(jnp.concatenate([low, high], axis=1)))
            field[:, 0:ny] += nu * u[:, 0:ny]
            field[:, last:] += nu * u[:, ny:]
        for copy in pending:
            copy.wait()
        acc = q_ref[r, 0]
        for j in range(1, members):
            acc = acc + q_ref[r, j]
        total[...] = acc
        smooth = stacked(smoothed(r))
        smooth = jnp.concatenate([smooth, jnp.zeros((pad, nx * ny), BF16)], axis=0)
        lifted = dot(lift_w[...], smooth)
        for x in range(nx):
            cols = slice(x * ny, (x + 1) * ny)
            field[:, cols] += anom32[pl.ds(x, state, stride=nx), :] * lifted[:, cols]
        if r > 0:
            for copy in halo:
                copy.wait()
            field[:, 0:ny] += nu * u_ref[r, 0]
            field[:, (nx - 1) * ny :] += nu * u_ref[r, nx + 1]
    for x in range(nx):
        out_ref[pl.ds(x, state, stride=nx), :] = field[:, x * ny : (x + 1) * ny]


def per_device(members, tiles, innovations, obs_column, physics, diffusion, anomalies, modes, bands):
    _, steps, state, obs = innovations.shape
    _, _, nx, ny = anomalies.shape
    count = modes.shape[1]
    rounds = steps - 1
    vmem = pl.BlockSpec(memory_space=pltpu.VMEM)
    hbm = pl.BlockSpec(memory_space=pl.ANY)
    out = pl.pallas_call(
        functools.partial(kernel, members, tiles),
        out_shape=jax.ShapeDtypeStruct((state * nx, ny), F32),
        in_specs=[pl.BlockSpec(memory_space=pltpu.SMEM), vmem, vmem, vmem, hbm, hbm, hbm],
        out_specs=vmem,
        scratch_shapes=[
            pltpu.VMEM((rounds, state, state), F32),
            pltpu.VMEM((steps, obs, state), BF16),
            pltpu.VMEM((state * nx, ny), BF16),
            pltpu.VMEM((state * nx, ny), F32),
            pltpu.VMEM((rounds, state, 3 * state), BF16),
            pltpu.VMEM((state, nx * ny), F32),
            pltpu.VMEM((state, ny), F32),
            pltpu.VMEM((state, ny), BF16),
            pltpu.VMEM((2 * count, state), BF16),
            pltpu.VMEM((2 * REACH + 1, count, ny), F32),
            pltpu.VMEM((3, obs, state), F32),
            pltpu.VMEM((2, steps, obs), jnp.int32),
            pltpu.VMEM((rounds, nx + 2, state, ny), F32),
            pltpu.VMEM((rounds, members, count, nx * ny), F32),
            pltpu.VMEM((count, nx * ny), F32),
            pltpu.SemaphoreType.DMA((3,)),
            pltpu.SemaphoreType.DMA((2,)),
            pltpu.SemaphoreType.DMA((2,)),
            pltpu.SemaphoreType.DMA((2,)),
            pltpu.SemaphoreType.DMA((2,)),
            pltpu.SemaphoreType.DMA((rounds, 2)),
            pltpu.SemaphoreType.DMA((rounds, 2)),
            pltpu.SemaphoreType.DMA((rounds, members)),
            pltpu.SemaphoreType.DMA((rounds, members)),
        ],
        compiler_params=pltpu.CompilerParams(
            collective_id=0, has_side_effects=True, vmem_limit_bytes=40 * 1024 * 1024
        ),
    )(
        bands, obs_column, diffusion.reshape(1, state), modes.T, physics,
        innovations.swapaxes(2, 3),
        anomalies.reshape(state * nx, ny),
    )
    return out.reshape(1, state, nx, ny)


def solution(mesh):
    in_specs = (
        P("member", None, None, "tile"),
        P(None, "tile"),
        P(),
        P(),
        P("member", None, "tile", None),
        P(),
        P(),
    )
    out_specs = P("member", None, "tile", None)
    return jax.shard_map(
        functools.partial(per_device, mesh.shape["member"], mesh.shape["tile"]),
        mesh=mesh, in_specs=in_specs, out_specs=out_specs, check_vma=False,
    )
```

```python
import functools

import jax
import jax.numpy as jnp
from jax import lax
from jax.experimental import pallas as pl
from jax.experimental.pallas import tpu as pltpu
from jax.sharding import PartitionSpec as P

REACH = 8
MESH = pl.DeviceIdType.MESH
F32 = jnp.float32
BF16 = jnp.bfloat16


def split(x):
    hi = x.astype(BF16)
    return hi, (x - hi.astype(F32)).astype(BF16)


def dot(a, b):
    return jnp.dot(a, b, preferred_element_type=F32)


def stacked(x):
    hi, lo = split(x)
    return jnp.concatenate([hi, lo, hi], axis=0)


def spread_obs(profile, obs_row, first, count):
    shape = (count, obs_row.shape[-1])
    column = lax.broadcasted_iota(jnp.int32, shape, 0) + first
    onehot = jnp.where(column == obs_row, 1.0, 0.0).astype(BF16)
    return lax.dot_general(
        profile, onehot, (((0,), (1,)), ((), ())), preferred_element_type=F32
    )


def kernel(
    members, tiles, bands_hbm, obs_hbm, diff_hbm, modes_hbm, phys_ref, innov_ref, anom_ref,
    out_ref,
    bands_ref, obs_ref, diff_ref, modes_ref, phys, innov, anom, anom32, weight, field, nu_ref, lift_w, proj_w, smooth_w,
    edge, edge_obs, u_ref, q_ref, total,
    local_sem, edge_send, edge_recv, obs_send, obs_recv, u_send, u_recv, q_send, q_recv,
):
    steps, obs, state = innov.shape
    ny = anom.shape[1]
    nx = anom.shape[0] // state
    modes = modes_ref.shape[0]
    rounds = steps - 1
    me = lax.axis_index("member")
    tile = lax.axis_index("tile")
    after = lax.rem(tile + 1, tiles)
    before = lax.rem(tile + tiles - 1, tiles)

    get_innov = pltpu.make_async_copy(innov_ref.at[0], innov, local_sem.at[0])
    get_phys = pltpu.make_async_copy(phys_ref.at[pl.ds(0, rounds)], phys, local_sem.at[1])
    get_anom = pltpu.make_async_copy(anom_ref, anom, local_sem.at[2])
    get_obs = pltpu.make_async_copy(obs_hbm, obs_ref, local_sem.at[3])
    get_modes = pltpu.make_async_copy(modes_hbm, modes_ref, local_sem.at[4])
    get_bands = pltpu.make_async_copy(bands_hbm, bands_ref, local_sem.at[5])
    get_diff = pltpu.make_async_copy(diff_hbm, diff_ref, local_sem.at[6])
    for get in (get_innov, get_obs, get_modes, get_anom, get_phys, get_bands, get_diff):
        get.start()

    barrier = pltpu.get_barrier_semaphore()
    for near in (before, after):
        pl.semaphore_signal(barrier, inc=1, device_id={"tile": near}, device_id_type=MESH)
    for j in range(1, members):
        peer = lax.rem(me + j, members)
        pl.semaphore_signal(barrier, inc=1, device_id={"member": peer}, device_id_type=MESH)

    get_innov.wait()
    edge[0] = innov[rounds].astype(F32)
    get_obs.wait()
    pl.semaphore_wait(barrier, members + 1)

    edge_copies = []
    for side, near in ((0, after), (1, before)):
        edge_copies.append(pltpu.make_async_remote_copy(
            edge.at[0], edge.at[1 + side], edge_send.at[side], edge_recv.at[side],
            device_id={"tile": near}, device_id_type=MESH))
        edge_copies.append(pltpu.make_async_remote_copy(
            obs_ref, edge_obs.at[side], obs_send.at[side], obs_recv.at[side],
            device_id={"tile": near}, device_id_type=MESH))
    for copy in edge_copies:
        copy.start()

    obs_all = obs_ref[...]
    field[...] = spread_obs(innov[rounds], obs_all[rounds : rounds + 1], 0, nx * ny)

    get_modes.wait()
    hi, lo = split(modes_ref[...])
    proj_w[...] = jnp.concatenate([hi, lo], axis=0)
    parts = jnp.concatenate([hi, hi, lo], axis=0).astype(F32)
    pad = lift_w.shape[1] - 3 * modes
    lift_w[...] = jnp.concatenate([parts, jnp.zeros((pad, state), F32)], axis=0).T.astype(BF16)

    get_anom.wait()
    anom32[...] = anom[...].astype(F32)

    def project_and_send(r):
        hi_cols, lo_cols = [], []
        for x in range(nx):
            cols = slice(x * ny, (x + 1) * ny)
            a, b = split(anom32[pl.ds(x, state, stride=nx), :] * field[:, cols])
            hi_cols.append(a)
            lo_cols.append(b)
        both = dot(proj_w[...], jnp.concatenate(hi_cols, axis=1))
        low = dot(proj_w[0:modes], jnp.concatenate(lo_cols, axis=1))
        q_ref[r, 0] = both[0:modes] + both[modes:] + low
        copies = []
        for j in range(1, members):
            copies.append(pltpu.make_async_remote_copy(
                q_ref.at[r, 0], q_ref.at[r, j], q_send.at[r, j], q_recv.at[r, j],
                device_id={"member": lax.rem(me + j, members)}, device_id_type=MESH))
        for copy in copies:
            copy.start()
        return copies

    pending = project_and_send(0)

    row = lax.broadcasted_iota(jnp.int32, (modes, ny), 0)
    lane = lax.broadcasted_iota(jnp.int32, (modes, ny), 1)
    bands = jnp.zeros((modes, ny), jnp.int32)
    get_bands.wait()
    for k in range(modes):
        bands = jnp.where(row == k, bands_ref[k], bands)
    scale = 1.0 / ((2 * bands + 1).astype(F32) * F32(members - 1))
    for i, d in enumerate(range(-REACH, REACH + 1)):
        ok = (abs(d) <= bands) & (lane + d >= 0) & (lane + d < ny)
        smooth_w[i] = jnp.where(ok, scale, 0.0)

    get_diff.wait()
    nu_ref[...] = jnp.broadcast_to(diff_ref[...], (ny, state)).T

    get_phys.wait()

    def physics_weights(t):
        hi, lo = split(phys[t].T)
        weight[t] = jnp.concatenate([hi, hi, lo], axis=1)

    physics_weights(rounds - 1)

    def smoothed(r):
        rows = []
        for x in range(nx):
            cols = slice(x * ny, (x + 1) * ny)
            q = total[:, cols]
            acc = smooth_w[REACH] * q
            for i, d in enumerate(range(-REACH, REACH + 1)):
                if d != 0:
                    acc = acc + smooth_w[i] * pltpu.roll(q, (-d) % ny, 1)
            rows.append(acc)
        return jnp.concatenate(rows, axis=1)

    lane_y = lax.broadcasted_iota(jnp.int32, (state, ny), 1)

    for r in range(rounds):
        t = rounds - 1 - r
        halo = []
        if r > 0:
            outer = jnp.concatenate([field[:, 0:ny], field[:, (nx - 1) * ny :]], axis=1)
            u = dot(weight[t], stacked(outer))
            u_ref[r, 1] = u[:, 0:ny]
            u_ref[r, nx] = u[:, ny:]
            halo = [
                pltpu.make_async_remote_copy(
                    u_ref.at[r, 1], u_ref.at[r, nx + 1], u_send.at[r, 0], u_recv.at[r, 0],
                    device_id={"tile": before}, device_id_type=MESH),
                pltpu.make_async_remote_copy(
                    u_ref.at[r, nx], u_ref.at[r, 0], u_send.at[r, 1], u_recv.at[r, 1],
                    device_id={"tile": after}, device_id_type=MESH),
            ]
            for copy in halo:
                copy.start()
            pending = project_and_send(r)
            u = dot(weight[t], stacked(field[:, ny : (nx - 1) * ny]))
            for x in range(1, nx - 1):
                u_ref[r, 1 + x] = u[:, (x - 1) * ny : x * ny]
        else:
            u = dot(weight[t], stacked(field[...]))
            for x in range(nx):
                u_ref[r, 1 + x] = u[:, x * ny : (x + 1) * ny]
        if t > 0:
            physics_weights(t - 1)
        nu = nu_ref[...]
        field[...] = spread_obs(innov[t], obs_all[t : t + 1], 0, nx * ny)
        for x in range(nx):
            cols = slice(x * ny, (x + 1) * ny)
            mid = u_ref[r, 1 + x]
            beside = jnp.where(lane_y == 0, 0.0, pltpu.roll(mid, 1, 1))
            beside = beside + jnp.where(lane_y == ny - 1, 0.0, pltpu.roll(mid, ny - 1, 1))
            if x > 0:
                beside = beside + u_ref[r, x]
            if x < nx - 1:
                beside = beside + u_ref[r, x + 2]
            field[:, cols] += mid + nu * (beside - 4.0 * mid)
        if r == 0:
            for copy in edge_copies:
                copy.wait()
            last = (nx - 1) * ny
            low = spread_obs(edge[1].astype(BF16), edge_obs[0, rounds : rounds + 1], last, ny)
            high = spread_obs(edge[2].astype(BF16), edge_obs[1, rounds : rounds + 1], 0, ny)
            u = dot(weight[t], stacked(jnp.concatenate([low, high], axis=1)))
            field[:, 0:ny] += nu * u[:, 0:ny]
            field[:, last:] += nu * u[:, ny:]
        for copy in pending:
            copy.wait()
        acc = q_ref[r, 0]
        for j in range(1, members):
            acc = acc + q_ref[r, j]
        total[...] = acc
        smooth = stacked(smoothed(r))
        smooth = jnp.concatenate([smooth, jnp.zeros((pad, nx * ny), BF16)], axis=0)
        lifted = dot(lift_w[...], smooth)
        for x in range(nx):
            cols = slice(x * ny, (x + 1) * ny)
            field[:, cols] += anom32[pl.ds(x, state, stride=nx), :] * lifted[:, cols]
        if r > 0:
            for copy in halo:
                copy.wait()
            field[:, 0:ny] += nu * u_ref[r, 0]
            field[:, (nx - 1) * ny :] += nu * u_ref[r, nx + 1]
    for x in range(nx):
        out_ref[pl.ds(x, state, stride=nx), :] = field[:, x * ny : (x + 1) * ny]


def per_device(members, tiles, innovations, obs_column, physics, diffusion, anomalies, modes, bands):
    _, steps, state, obs = innovations.shape
    _, _, nx, ny = anomalies.shape
    count = modes.shape[1]
    rounds = steps - 1
    vmem = pl.BlockSpec(memory_space=pltpu.VMEM)
    hbm = pl.BlockSpec(memory_space=pl.ANY)
    out = pl.pallas_call(
        functools.partial(kernel, members, tiles),
        out_shape=jax.ShapeDtypeStruct((state * nx, ny), F32),
        in_specs=[hbm] * 7,
        out_specs=vmem,
        scratch_shapes=[
            pltpu.SMEM((count,), jnp.int32),
            pltpu.VMEM((steps, obs), jnp.int32),
            pltpu.VMEM((1, state), F32),
            pltpu.VMEM((count, state), F32),
            pltpu.VMEM((rounds, state, state), F32),
            pltpu.VMEM((steps, obs, state), BF16),
            pltpu.VMEM((state * nx, ny), BF16),
            pltpu.VMEM((state * nx, ny), F32),
            pltpu.VMEM((rounds, state, 3 * state), BF16),
            pltpu.VMEM((state, nx * ny), F32),
            pltpu.VMEM((state, ny), F32),
            pltpu.VMEM((state, ny), BF16),
            pltpu.VMEM((2 * count, state), BF16),
            pltpu.VMEM((2 * REACH + 1, count, ny), F32),
            pltpu.VMEM((3, obs, state), F32),
            pltpu.VMEM((2, steps, obs), jnp.int32),
            pltpu.VMEM((rounds, nx + 2, state, ny), F32),
            pltpu.VMEM((rounds, members, count, nx * ny), F32),
            pltpu.VMEM((count, nx * ny), F32),
            pltpu.SemaphoreType.DMA((7,)),
            pltpu.SemaphoreType.DMA((2,)),
            pltpu.SemaphoreType.DMA((2,)),
            pltpu.SemaphoreType.DMA((2,)),
            pltpu.SemaphoreType.DMA((2,)),
            pltpu.SemaphoreType.DMA((rounds, 2)),
            pltpu.SemaphoreType.DMA((rounds, 2)),
            pltpu.SemaphoreType.DMA((rounds, members)),
            pltpu.SemaphoreType.DMA((rounds, members)),
        ],
        compiler_params=pltpu.CompilerParams(
            collective_id=0, has_side_effects=True, vmem_limit_bytes=60 * 1024 * 1024
        ),
    )(
        bands, obs_column, diffusion.reshape(1, state), modes.T, physics,
        innovations.swapaxes(2, 3),
        anomalies.reshape(state * nx, ny),
    )
    return out.reshape(1, state, nx, ny)


def solution(mesh):
    in_specs = (
        P("member", None, None, "tile"),
        P(None, "tile"),
        P(),
        P(),
        P("member", None, "tile", None),
        P(),
        P(),
    )
    out_specs = P("member", None, "tile", None)
    return jax.shard_map(
        functools.partial(per_device, mesh.shape["member"], mesh.shape["tile"]),
        mesh=mesh, in_specs=in_specs, out_specs=out_specs, check_vma=False,
    )
```

```python
import functools

import jax
import jax.numpy as jnp
from jax import lax
from jax.experimental import pallas as pl
from jax.experimental.pallas import tpu as pltpu
from jax.sharding import PartitionSpec as P

REACH = 8
MESH = pl.DeviceIdType.MESH
F32 = jnp.float32
BF16 = jnp.bfloat16


def split(x):
    hi = x.astype(BF16)
    return hi, (x - hi.astype(F32)).astype(BF16)


def dot(a, b):
    return jnp.dot(a, b, preferred_element_type=F32)


def stacked(x):
    hi, lo = split(x)
    return jnp.concatenate([hi, lo, hi], axis=0)


def spread_obs(profile, obs_row, first, count):
    shape = (count, obs_row.shape[-1])
    column = lax.broadcasted_iota(jnp.int32, shape, 0) + first
    onehot = jnp.where(column == obs_row, 1.0, 0.0).astype(BF16)
    return lax.dot_general(
        profile, onehot, (((0,), (1,)), ((), ())), preferred_element_type=F32
    )


def kernel(
    members, tiles, bands_hbm, obs_hbm, diff_hbm, modes_hbm, phys_ref, innov_ref, anom_ref,
    out_ref,
    bands_ref, obs_ref, diff_ref, modes_ref, phys, innov, anom, anom32, weight, field, nu_ref, lift_w, proj_w, smooth_w,
    edge, edge_obs, u_ref, halo_out, halo_in, q_ref, total,
    local_sem, edge_send, edge_recv, obs_send, obs_recv, u_send, u_recv, q_send, q_recv,
):
    steps, obs, state = innov.shape
    ny = anom.shape[1]
    nx = anom.shape[0] // state
    modes = modes_ref.shape[0]
    rounds = steps - 1
    me = lax.axis_index("member")
    tile = lax.axis_index("tile")
    after = lax.rem(tile + 1, tiles)
    before = lax.rem(tile + tiles - 1, tiles)

    get_innov = pltpu.make_async_copy(innov_ref.at[0], innov, local_sem.at[0])
    get_phys = pltpu.make_async_copy(phys_ref.at[pl.ds(0, rounds)], phys, local_sem.at[1])
    get_anom = pltpu.make_async_copy(anom_ref, anom, local_sem.at[2])
    get_obs = pltpu.make_async_copy(obs_hbm, obs_ref, local_sem.at[3])
    get_modes = pltpu.make_async_copy(modes_hbm, modes_ref, local_sem.at[4])
    get_bands = pltpu.make_async_copy(bands_hbm, bands_ref, local_sem.at[5])
    get_diff = pltpu.make_async_copy(diff_hbm, diff_ref, local_sem.at[6])
    for get in (get_innov, get_obs, get_modes, get_anom, get_phys, get_bands, get_diff):
        get.start()

    barrier = pltpu.get_barrier_semaphore()
    for near in (before, after):
        pl.semaphore_signal(barrier, inc=1, device_id={"tile": near}, device_id_type=MESH)
    for j in range(1, members):
        peer = lax.rem(me + j, members)
        pl.semaphore_signal(barrier, inc=1, device_id={"member": peer}, device_id_type=MESH)

    get_innov.wait()
    edge[0] = innov[rounds].astype(F32)
    get_obs.wait()
    pl.semaphore_wait(barrier, members + 1)

    edge_copies = []
    for side, near in ((0, after), (1, before)):
        edge_copies.append(pltpu.make_async_remote_copy(
            edge.at[0], edge.at[1 + side], edge_send.at[side], edge_recv.at[side],
            device_id={"tile": near}, device_id_type=MESH))
        edge_copies.append(pltpu.make_async_remote_copy(
            obs_ref, edge_obs.at[side], obs_send.at[side], obs_recv.at[side],
            device_id={"tile": near}, device_id_type=MESH))
    for copy in edge_copies:
        copy.start()

    obs_all = obs_ref[...]
    field[...] = spread_obs(innov[rounds], obs_all[rounds : rounds + 1], 0, nx * ny)

    get_modes.wait()
    hi, lo = split(modes_ref[...])
    proj_w[...] = jnp.concatenate([hi, lo], axis=0)
    parts = jnp.concatenate([hi, hi, lo], axis=0).astype(F32)
    pad = lift_w.shape[1] - 3 * modes
    lift_w[...] = jnp.concatenate([parts, jnp.zeros((pad, state), F32)], axis=0).T.astype(BF16)

    get_anom.wait()
    anom32[...] = anom[...].astype(F32)

    def project_and_send(r):
        hi_cols, lo_cols = [], []
        for x in range(nx):
            cols = slice(x * ny, (x + 1) * ny)
            a, b = split(anom32[pl.ds(x, state, stride=nx), :] * field[:, cols])
            hi_cols.append(a)
            lo_cols.append(b)
        both = dot(proj_w[...], jnp.concatenate(hi_cols, axis=1))
        low = dot(proj_w[0:modes], jnp.concatenate(lo_cols, axis=1))
        q_ref[r, 0] = both[0:modes] + both[modes:] + low
        copies = []
        for j in range(1, members):
            copies.append(pltpu.make_async_remote_copy(
                q_ref.at[r, 0], q_ref.at[r, j], q_send.at[r, j], q_recv.at[r, j],
                device_id={"member": lax.rem(me + j, members)}, device_id_type=MESH))
        for copy in copies:
            copy.start()
        return copies

    pending = project_and_send(0)

    row = lax.broadcasted_iota(jnp.int32, (modes, ny), 0)
    lane = lax.broadcasted_iota(jnp.int32, (modes, ny), 1)
    bands = jnp.zeros((modes, ny), jnp.int32)
    get_bands.wait()
    for k in range(modes):
        bands = jnp.where(row == k, bands_ref[k], bands)
    scale = 1.0 / ((2 * bands + 1).astype(F32) * F32(members - 1))
    for i, d in enumerate(range(-REACH, REACH + 1)):
        ok = (abs(d) <= bands) & (lane + d >= 0) & (lane + d < ny)
        smooth_w[i] = jnp.where(ok, scale, 0.0)

    get_diff.wait()
    nu_ref[...] = jnp.broadcast_to(diff_ref[...], (ny, state)).T

    get_phys.wait()

    def physics_weights(t):
        hi, lo = split(phys[t].T)
        weight[t] = jnp.concatenate([hi, hi, lo], axis=1)

    physics_weights(rounds - 1)

    def smoothed(r):
        rows = []
        for x in range(nx):
            cols = slice(x * ny, (x + 1) * ny)
            q = total[:, cols]
            acc = smooth_w[REACH] * q
            for i, d in enumerate(range(-REACH, REACH + 1)):
                if d != 0:
                    acc = acc + smooth_w[i] * pltpu.roll(q, (-d) % ny, 1)
            rows.append(acc)
        return jnp.concatenate(rows, axis=1)

    lane_y = lax.broadcasted_iota(jnp.int32, (state, ny), 1)

    half = ny // 2
    lower = lax.broadcasted_iota(jnp.int32, (state, ny), 1) < half
    last = (nx - 1) * ny
    unsent = []

    def trade(a, b):
        keep = lower[0 : a.shape[0]]
        first = jnp.where(keep, a, pltpu.roll(b, half, 1))
        return first, jnp.where(keep, pltpu.roll(a, half, 1), b)

    def send_part(r, part, layers):
        u = dot(weight[rounds - 1 - r], stacked(layers))
        left, right = trade(u[0 : state // 2], u[state // 2 :])
        halo_out[r, part, 0] = left
        halo_out[r, part, 1] = right
        copies = [
            pltpu.make_async_remote_copy(
                halo_out.at[r, part, side], halo_in.at[r, part, 1 - side],
                u_send.at[r, part, side], u_recv.at[r, part, 1 - side],
                device_id={"tile": near}, device_id_type=MESH)
            for side, near in ((0, before), (1, after))
        ]
        for copy in copies:
            copy.start()
        unsent.extend(copies)
        return u, copies

    sent = []
    for r in range(rounds):
        t = rounds - 1 - r
        if r > 0:
            pending = project_and_send(r)
            u_ref[r, 1], u_ref[r, nx] = trade(sent[0][0], sent[1][0])
            u = dot(weight[t], stacked(field[:, ny:last]))
            for x in range(1, nx - 1):
                u_ref[r, 1 + x] = u[:, (x - 1) * ny : x * ny]
        else:
            u = dot(weight[t], stacked(field[...]))
            for x in range(nx):
                u_ref[r, 1 + x] = u[:, x * ny : (x + 1) * ny]
        if t > 0:
            physics_weights(t - 1)
        nu = nu_ref[...]
        field[...] = spread_obs(innov[t], obs_all[t : t + 1], 0, nx * ny)
        for x in range(nx):
            cols = slice(x * ny, (x + 1) * ny)
            mid = u_ref[r, 1 + x]
            beside = jnp.where(lane_y == 0, 0.0, pltpu.roll(mid, 1, 1))
            beside = beside + jnp.where(lane_y == ny - 1, 0.0, pltpu.roll(mid, ny - 1, 1))
            if x > 0:
                beside = beside + u_ref[r, x]
            if x < nx - 1:
                beside = beside + u_ref[r, x + 2]
            field[:, cols] += mid + nu * (beside - 4.0 * mid)
        if r == 0:
            for copy in edge_copies:
                copy.wait()
            low = spread_obs(edge[1].astype(BF16), edge_obs[0, rounds : rounds + 1], last, ny)
            high = spread_obs(edge[2].astype(BF16), edge_obs[1, rounds : rounds + 1], 0, ny)
            u = dot(weight[t], stacked(jnp.concatenate([low, high], axis=1)))
            field[:, 0:ny] += nu * u[:, 0:ny]
            field[:, last:] += nu * u[:, ny:]
        for copy in pending:
            copy.wait()
        acc = q_ref[r, 0]
        for j in range(1, members):
            acc = acc + q_ref[r, j]
        total[...] = acc
        smooth = stacked(smoothed(r))
        smooth = jnp.concatenate([smooth, jnp.zeros((pad, nx * ny), BF16)], axis=0)
        lifted = dot(lift_w[...], smooth)
        for x in range(nx):
            cols = slice(x * ny, (x + 1) * ny)
            field[:, cols] += anom32[pl.ds(x, state, stride=nx), :] * lifted[:, cols]
        layers = list(trade(field[:, 0:ny], field[:, last:]))
        arriving, sent = sent, []
        for part in range(2):
            if r > 0:
                for copy in arriving[part][1]:
                    copy.wait_recv()
                outside = trade(halo_in[r, part, 0], halo_in[r, part, 1])
                layers[part] = layers[part] + nu * jnp.concatenate(outside, axis=0)
            if r < rounds - 1:
                sent.append(send_part(r + 1, part, layers[part]))
        if r > 0:
            field[:, 0:ny], field[:, last:] = trade(*layers)
    for copy in unsent:
        copy.wait_send()
    for x in range(nx):
        out_ref[pl.ds(x, state, stride=nx), :] = field[:, x * ny : (x + 1) * ny]


def per_device(members, tiles, innovations, obs_column, physics, diffusion, anomalies, modes, bands):
    _, steps, state, obs = innovations.shape
    _, _, nx, ny = anomalies.shape
    count = modes.shape[1]
    rounds = steps - 1
    vmem = pl.BlockSpec(memory_space=pltpu.VMEM)
    hbm = pl.BlockSpec(memory_space=pl.ANY)
    out = pl.pallas_call(
        functools.partial(kernel, members, tiles),
        out_shape=jax.ShapeDtypeStruct((state * nx, ny), F32),
        in_specs=[hbm] * 7,
        out_specs=vmem,
        scratch_shapes=[
            pltpu.SMEM((count,), jnp.int32),
            pltpu.VMEM((steps, obs), jnp.int32),
            pltpu.VMEM((1, state), F32),
            pltpu.VMEM((count, state), F32),
            pltpu.VMEM((rounds, state, state), F32),
            pltpu.VMEM((steps, obs, state), BF16),
            pltpu.VMEM((state * nx, ny), BF16),
            pltpu.VMEM((state * nx, ny), F32),
            pltpu.VMEM((rounds, state, 3 * state), BF16),
            pltpu.VMEM((state, nx * ny), F32),
            pltpu.VMEM((state, ny), F32),
            pltpu.VMEM((state, ny), BF16),
            pltpu.VMEM((2 * count, state), BF16),
            pltpu.VMEM((2 * REACH + 1, count, ny), F32),
            pltpu.VMEM((3, obs, state), F32),
            pltpu.VMEM((2, steps, obs), jnp.int32),
            pltpu.VMEM((rounds, nx + 2, state, ny), F32),
            pltpu.VMEM((rounds, 2, 2, state // 2, ny), F32),
            pltpu.VMEM((rounds, 2, 2, state // 2, ny), F32),
            pltpu.VMEM((rounds, members, count, nx * ny), F32),
            pltpu.VMEM((count, nx * ny), F32),
            pltpu.SemaphoreType.DMA((7,)),
            pltpu.SemaphoreType.DMA((2,)),
            pltpu.SemaphoreType.DMA((2,)),
            pltpu.SemaphoreType.DMA((2,)),
            pltpu.SemaphoreType.DMA((2,)),
            pltpu.SemaphoreType.DMA((rounds, 2, 2)),
            pltpu.SemaphoreType.DMA((rounds, 2, 2)),
            pltpu.SemaphoreType.DMA((rounds, members)),
            pltpu.SemaphoreType.DMA((rounds, members)),
        ],
        compiler_params=pltpu.CompilerParams(
            collective_id=0, has_side_effects=True, vmem_limit_bytes=60 * 1024 * 1024
        ),
    )(
        bands, obs_column, diffusion.reshape(1, state), modes.T, physics,
        innovations.swapaxes(2, 3),
        anomalies.reshape(state * nx, ny),
    )
    return out.reshape(1, state, nx, ny)


def solution(mesh):
    in_specs = (
        P("member", None, None, "tile"),
        P(None, "tile"),
        P(),
        P(),
        P("member", None, "tile", None),
        P(),
        P(),
    )
    out_specs = P("member", None, "tile", None)
    return jax.shard_map(
        functools.partial(per_device, mesh.shape["member"], mesh.shape["tile"]),
        mesh=mesh, in_specs=in_specs, out_specs=out_specs, check_vma=False,
    )
```

```python
import functools

import jax
import jax.numpy as jnp
from jax import lax
from jax.experimental import pallas as pl
from jax.experimental.pallas import tpu as pltpu
from jax.sharding import PartitionSpec as P

REACH = 8
MESH = pl.DeviceIdType.MESH
F32 = jnp.float32
BF16 = jnp.bfloat16


def split(x):
    hi = x.astype(BF16)
    return hi, (x - hi.astype(F32)).astype(BF16)


def dot(a, b):
    return jnp.dot(a, b, preferred_element_type=F32)


def stacked(x):
    hi, lo = split(x)
    return jnp.concatenate([hi, lo, hi], axis=0)


def spread_obs(profile, obs_row, first, count):
    shape = (count, obs_row.shape[-1])
    column = lax.broadcasted_iota(jnp.int32, shape, 0) + first
    onehot = jnp.where(column == obs_row, 1.0, 0.0).astype(BF16)
    return lax.dot_general(
        profile, onehot, (((0,), (1,)), ((), ())), preferred_element_type=F32
    )


def kernel(
    members, tiles, bands_hbm, obs_hbm, diff_hbm, modes_hbm, phys_ref, innov_ref, anom_ref,
    out_ref,
    bands_ref, obs_ref, diff_ref, modes_ref, phys, innov, anom, anom32, weight, field, nu_ref, lift_w, proj_w, smooth_w,
    edge, edge_obs, u_ref, halo_out, halo_in, own, q_ref, total,
    local_sem, edge_send, edge_recv, obs_send, obs_recv, u_send, u_recv, q_send, q_recv, t_send, t_recv,
):
    steps, obs, state = innov.shape
    ny = anom.shape[1]
    nx = anom.shape[0] // state
    modes = modes_ref.shape[0]
    rounds = steps - 1
    share = modes * nx // members
    me = lax.axis_index("member")
    tile = lax.axis_index("tile")
    after = lax.rem(tile + 1, tiles)
    before = lax.rem(tile + tiles - 1, tiles)

    get_innov = pltpu.make_async_copy(innov_ref.at[0], innov, local_sem.at[0])
    get_phys = pltpu.make_async_copy(phys_ref.at[pl.ds(0, rounds)], phys, local_sem.at[1])
    get_anom = pltpu.make_async_copy(anom_ref, anom, local_sem.at[2])
    get_obs = pltpu.make_async_copy(obs_hbm, obs_ref, local_sem.at[3])
    get_modes = pltpu.make_async_copy(modes_hbm, modes_ref, local_sem.at[4])
    get_bands = pltpu.make_async_copy(bands_hbm, bands_ref, local_sem.at[5])
    get_diff = pltpu.make_async_copy(diff_hbm, diff_ref, local_sem.at[6])
    for get in (get_innov, get_obs, get_modes, get_anom, get_phys, get_bands, get_diff):
        get.start()

    barrier = pltpu.get_barrier_semaphore()
    for near in (before, after):
        pl.semaphore_signal(barrier, inc=1, device_id={"tile": near}, device_id_type=MESH)
    for j in range(1, members):
        peer = lax.rem(me + j, members)
        pl.semaphore_signal(barrier, inc=1, device_id={"member": peer}, device_id_type=MESH)

    get_innov.wait()
    edge[0] = innov[rounds].astype(F32)
    get_obs.wait()
    pl.semaphore_wait(barrier, members + 1)

    edge_copies = []
    for side, near in ((0, after), (1, before)):
        edge_copies.append(pltpu.make_async_remote_copy(
            edge.at[0], edge.at[1 + side], edge_send.at[side], edge_recv.at[side],
            device_id={"tile": near}, device_id_type=MESH))
        edge_copies.append(pltpu.make_async_remote_copy(
            obs_ref, edge_obs.at[side], obs_send.at[side], obs_recv.at[side],
            device_id={"tile": near}, device_id_type=MESH))
    for copy in edge_copies:
        copy.start()

    obs_all = obs_ref[...]
    field[...] = spread_obs(innov[rounds], obs_all[rounds : rounds + 1], 0, nx * ny)

    get_modes.wait()
    hi, lo = split(modes_ref[...])
    proj_w[...] = jnp.concatenate([hi, lo], axis=0)
    parts = jnp.concatenate([hi, hi, lo], axis=0).astype(F32)
    pad = lift_w.shape[1] - 3 * modes
    lift_w[...] = jnp.concatenate([parts, jnp.zeros((pad, state), F32)], axis=0).T.astype(BF16)

    get_anom.wait()
    anom32[...] = anom[...].astype(F32)

    def project_and_send(r):
        hi_cols, lo_cols = [], []
        for x in range(nx):
            cols = slice(x * ny, (x + 1) * ny)
            a, b = split(anom32[pl.ds(x, state, stride=nx), :] * field[:, cols])
            hi_cols.append(a)
            lo_cols.append(b)
        both = dot(proj_w[...], jnp.concatenate(hi_cols, axis=1))
        low = dot(proj_w[0:modes], jnp.concatenate(lo_cols, axis=1))
        q = both[0:modes] + both[modes:] + low
        q = jnp.concatenate([q[:, x * ny : (x + 1) * ny] for x in range(nx)], axis=0)
        for m in range(members):
            own[r, m] = q[m * share : (m + 1) * share]
        return to_peers(lambda peer, j: (own.at[r, peer], q_ref.at[r, j]), q_send.at[r], q_recv.at[r])

    def to_peers(refs, send, recv):
        copies = []
        for j in range(1, members):
            peer = lax.rem(me + j, members)
            src, dst = refs(peer, j)
            copies.append(pltpu.make_async_remote_copy(
                src, dst, send.at[j], recv.at[j],
                device_id={"member": peer}, device_id_type=MESH))
        for copy in copies:
            copy.start()
        return copies

    def add_and_return(r, copies):
        for copy in copies:
            copy.wait()
        acc = own[r, me]
        for j in range(1, members):
            acc = acc + q_ref[r, j]
        total[r, me] = acc
        return to_peers(lambda peer, j: (total.at[r, me], total.at[r, me]), t_send.at[r], t_recv.at[r])

    pending = project_and_send(0)

    row = lax.broadcasted_iota(jnp.int32, (modes, ny), 0)
    lane = lax.broadcasted_iota(jnp.int32, (modes, ny), 1)
    bands = jnp.zeros((modes, ny), jnp.int32)
    get_bands.wait()
    for k in range(modes):
        bands = jnp.where(row == k, bands_ref[k], bands)
    scale = 1.0 / ((2 * bands + 1).astype(F32) * F32(members - 1))
    for i, d in enumerate(range(-REACH, REACH + 1)):
        ok = (abs(d) <= bands) & (lane + d >= 0) & (lane + d < ny)
        smooth_w[i] = jnp.where(ok, scale, 0.0)

    get_diff.wait()
    nu_ref[...] = jnp.broadcast_to(diff_ref[...], (ny, state)).T

    get_phys.wait()

    def physics_weights(t):
        hi, lo = split(phys[t].T)
        weight[t] = jnp.concatenate([hi, hi, lo], axis=1)

    physics_weights(rounds - 1)

    def smoothed(r):
        rows = []
        sums = jnp.concatenate([total[r, m] for m in range(members)], axis=0)
        for x in range(nx):
            q = sums[x * modes : (x + 1) * modes]
            acc = smooth_w[REACH] * q
            for i, d in enumerate(range(-REACH, REACH + 1)):
                if d != 0:
                    acc = acc + smooth_w[i] * pltpu.roll(q, (-d) % ny, 1)
            rows.append(acc)
        return jnp.concatenate(rows, axis=1)

    lane_y = lax.broadcasted_iota(jnp.int32, (state, ny), 1)

    half = ny // 2
    lower = lax.broadcasted_iota(jnp.int32, (state, ny), 1) < half
    last = (nx - 1) * ny
    unsent = []

    def trade(a, b):
        keep = lower[0 : a.shape[0]]
        first = jnp.where(keep, a, pltpu.roll(b, half, 1))
        return first, jnp.where(keep, pltpu.roll(a, half, 1), b)

    def send_part(r, part, layers):
        u = dot(weight[rounds - 1 - r], stacked(layers))
        left, right = trade(u[0 : state // 2], u[state // 2 :])
        halo_out[r, part, 0] = left
        halo_out[r, part, 1] = right
        copies = [
            pltpu.make_async_remote_copy(
                halo_out.at[r, part, side], halo_in.at[r, part, 1 - side],
                u_send.at[r, part, side], u_recv.at[r, part, 1 - side],
                device_id={"tile": near}, device_id_type=MESH)
            for side, near in ((0, before), (1, after))
        ]
        for copy in copies:
            copy.start()
        unsent.extend(copies)
        return u, copies

    sent = []
    for r in range(rounds):
        t = rounds - 1 - r
        if r > 0:
            pending = project_and_send(r)
            u_ref[r, 1], u_ref[r, nx] = trade(sent[0][0], sent[1][0])
            u = dot(weight[t], stacked(field[:, ny:last]))
            for x in range(1, nx - 1):
                u_ref[r, 1 + x] = u[:, (x - 1) * ny : x * ny]
        else:
            u = dot(weight[t], stacked(field[...]))
            for x in range(nx):
                u_ref[r, 1 + x] = u[:, x * ny : (x + 1) * ny]
        pending = add_and_return(r, pending)
        if t > 0:
            physics_weights(t - 1)
        nu = nu_ref[...]
        field[...] = spread_obs(innov[t], obs_all[t : t + 1], 0, nx * ny)
        for x in range(nx):
            cols = slice(x * ny, (x + 1) * ny)
            mid = u_ref[r, 1 + x]
            beside = jnp.where(lane_y == 0, 0.0, pltpu.roll(mid, 1, 1))
            beside = beside + jnp.where(lane_y == ny - 1, 0.0, pltpu.roll(mid, ny - 1, 1))
            if x > 0:
                beside = beside + u_ref[r, x]
            if x < nx - 1:
                beside = beside + u_ref[r, x + 2]
            field[:, cols] += mid + nu * (beside - 4.0 * mid)
        if r == 0:
            for copy in edge_copies:
                copy.wait()
            low = spread_obs(edge[1].astype(BF16), edge_obs[0, rounds : rounds + 1], last, ny)
            high = spread_obs(edge[2].astype(BF16), edge_obs[1, rounds : rounds + 1], 0, ny)
            u = dot(weight[t], stacked(jnp.concatenate([low, high], axis=1)))
            field[:, 0:ny] += nu * u[:, 0:ny]
            field[:, last:] += nu * u[:, ny:]
        for copy in pending:
            copy.wait()
        smooth = stacked(smoothed(r))
        smooth = jnp.concatenate([smooth, jnp.zeros((pad, nx * ny), BF16)], axis=0)
        lifted = dot(lift_w[...], smooth)
        for x in range(nx):
            cols = slice(x * ny, (x + 1) * ny)
            field[:, cols] += anom32[pl.ds(x, state, stride=nx), :] * lifted[:, cols]
        layers = list(trade(field[:, 0:ny], field[:, last:]))
        arriving, sent = sent, []
        for part in range(2):
            if r > 0:
                for copy in arriving[part][1]:
                    copy.wait_recv()
                outside = trade(halo_in[r, part, 0], halo_in[r, part, 1])
                layers[part] = layers[part] + nu * jnp.concatenate(outside, axis=0)
            if r < rounds - 1:
                sent.append(send_part(r + 1, part, layers[part]))
        if r > 0:
            field[:, 0:ny], field[:, last:] = trade(*layers)
    for copy in unsent:
        copy.wait_send()
    for x in range(nx):
        out_ref[pl.ds(x, state, stride=nx), :] = field[:, x * ny : (x + 1) * ny]


def per_device(members, tiles, innovations, obs_column, physics, diffusion, anomalies, modes, bands):
    _, steps, state, obs = innovations.shape
    _, _, nx, ny = anomalies.shape
    count = modes.shape[1]
    rounds = steps - 1
    vmem = pl.BlockSpec(memory_space=pltpu.VMEM)
    hbm = pl.BlockSpec(memory_space=pl.ANY)
    out = pl.pallas_call(
        functools.partial(kernel, members, tiles),
        out_shape=jax.ShapeDtypeStruct((state * nx, ny), F32),
        in_specs=[hbm] * 7,
        out_specs=vmem,
        scratch_shapes=[
            pltpu.SMEM((count,), jnp.int32),
            pltpu.VMEM((steps, obs), jnp.int32),
            pltpu.VMEM((1, state), F32),
            pltpu.VMEM((count, state), F32),
            pltpu.VMEM((rounds, state, state), F32),
            pltpu.VMEM((steps, obs, state), BF16),
            pltpu.VMEM((state * nx, ny), BF16),
            pltpu.VMEM((state * nx, ny), F32),
            pltpu.VMEM((rounds, state, 3 * state), BF16),
            pltpu.VMEM((state, nx * ny), F32),
            pltpu.VMEM((state, ny), F32),
            pltpu.VMEM((state, ny), BF16),
            pltpu.VMEM((2 * count, state), BF16),
            pltpu.VMEM((2 * REACH + 1, count, ny), F32),
            pltpu.VMEM((3, obs, state), F32),
            pltpu.VMEM((2, steps, obs), jnp.int32),
            pltpu.VMEM((rounds, nx + 2, state, ny), F32),
            pltpu.VMEM((rounds, 2, 2, state // 2, ny), F32),
            pltpu.VMEM((rounds, 2, 2, state // 2, ny), F32),
            pltpu.VMEM((rounds, members, count * nx // members, ny), F32),
            pltpu.VMEM((rounds, members, count * nx // members, ny), F32),
            pltpu.VMEM((rounds, members, count * nx // members, ny), F32),
            pltpu.SemaphoreType.DMA((7,)),
            pltpu.SemaphoreType.DMA((2,)),
            pltpu.SemaphoreType.DMA((2,)),
            pltpu.SemaphoreType.DMA((2,)),
            pltpu.SemaphoreType.DMA((2,)),
            pltpu.SemaphoreType.DMA((rounds, 2, 2)),
            pltpu.SemaphoreType.DMA((rounds, 2, 2)),
            pltpu.SemaphoreType.DMA((rounds, members)),
            pltpu.SemaphoreType.DMA((rounds, members)),
            pltpu.SemaphoreType.DMA((rounds, members)),
            pltpu.SemaphoreType.DMA((rounds, members)),
        ],
        compiler_params=pltpu.CompilerParams(
            collective_id=0, has_side_effects=True, vmem_limit_bytes=60 * 1024 * 1024
        ),
    )(
        bands, obs_column, diffusion.reshape(1, state), modes.T, physics,
        innovations.swapaxes(2, 3),
        anomalies.reshape(state * nx, ny),
    )
    return out.reshape(1, state, nx, ny)


def solution(mesh):
    in_specs = (
        P("member", None, None, "tile"),
        P(None, "tile"),
        P(),
        P(),
        P("member", None, "tile", None),
        P(),
        P(),
    )
    out_specs = P("member", None, "tile", None)
    return jax.shard_map(
        functools.partial(per_device, mesh.shape["member"], mesh.shape["tile"]),
        mesh=mesh, in_specs=in_specs, out_specs=out_specs, check_vma=False,
    )
```
